32 devices in a mesh: dp: 4 (over x, core), row: 2 (over y), col: 4 (over z).
Axes of the slice: x: 2, y: 2, z: 4, core: 2. Of those that a mesh axis runs over, the one named last changes fastest.
Arguments:
- block_input: float32 [15760, 768], P(('dp', 'row'), 'col'), may hold values from -6 to 6
- ln1_gain: float32 [768], P('col'), may hold values from 0.25 to 1.75
- ln1_bias: float32 [768], P('col'), may hold values from -3 to 3
- qkv_weight: bfloat16 [768, 2304], P('row', 'col'), may hold values from -0.21875 to 0.21875
- out_weight: bfloat16 [768, 768], P('row', 'col'), may hold values from -1.75 to 1.75
- ln2_gain: float32 [768], P('col'), may hold values from 0.25 to 1.75
- ln2_bias: float32 [768], P('col'), may hold values from -3 to 3
- router_weight: bfloat16 [768, 32], P('col'), may hold values from -0.15625 to 0.15625
- expert_in: bfloat16 [32, 768, 3072], P('row', None, 'col'), may hold values from -0.21875 to 0.21875
- expert_out: bfloat16 [32, 3072, 768], P('row', 'col'), may hold values from -1.25 to 1.25
- expert_ids: int32 [15760, 2], P(('dp', 'row')), may hold values from 0 to 31, all different within a row; in each aligned block of 1970 rows (0 to 1969, 1970 to 3939, ...) at most 168 rows name the same one
- kept_flags: int32 [15760, 2], P(('dp', 'row')), may hold values 0 or 1
- cotangent: float32 [15760, 768], P(('dp', 'row'), 'col'), may hold values from -6 to 6
Outputs:
- output: float32 [15760, 768], P(('dp', 'row'), 'col')
- grad_input: float32 [15760, 768], P(('dp', 'row'), 'col')
- grad_qkv: float32 [768, 2304], P('row', 'col')
- grad_proj: float32 [768, 768], P('row', 'col')
- grad_router: float32 [768, 32], P('col')
- grad_expert_in: float32 [32, 768, 3072], P('row', None, 'col')
- grad_expert_out: float32 [32, 3072, 768], P('row', 'col')
- grad_ln1_gain: float32 [768], P('col')
- grad_ln1_bias: float32 [768], P('col')
- grad_ln2_gain: float32 [768], P('col')
- grad_ln2_bias: float32 [768], P('col')
The draws below stay inside these ranges and needn't reach their ends.
Inputs may be any that keep to these rules, and one draw needn't show every extreme that they name: `expert_ids`: each token names two different experts. Among the routes of the 1970 rows of one device (aligned blocks), no expert is named more than 168 times, and in some block one expert is named exactly 168 times.
All inputs are finite; a program needn't handle non-finite values. No bound on the sum of `kept_flags` on one device may be relied on, other than what follows from the above.
Results may differ from the reference program's by a relative error of at most 0.015.
Values may be sent and summed in bfloat16 or wider, within the bound.
A program may use at most 320 MiB of HBM per device.

```python
import math
from functools import partial
import jax
import jax.numpy as jnp
import numpy as np
from jax import lax

D = 768
HEADS = 12
HEAD_DIM = 64
FF = 3072
E = 32
SEQ = 197
IMG_DEV = 10
CAP = 168
TOKENS = 15760


def with_ends(drawn, own_key, low, top_value):
    shape = drawn.shape
    index_at = [jax.random.randint(jax.random.fold_in(own_key, axis), (), 0, shape[axis]) for axis in range(len(shape))]
    drawn = drawn.at[tuple(index_at)].set(low)
    longest = shape.index(max(shape))
    index_at[longest] = (index_at[longest] + 1) % shape[longest]
    return drawn.at[tuple(index_at)].set(top_value)


def shard_levels(rng, extent, split, low, high):
    loudness = 1.0
    for position, shards_of in split:
        heights = jax.random.uniform(jax.random.fold_in(jax.random.fold_in(rng, 6), position), (shards_of,), jnp.float32, low / len(split), high / len(split))
        loudness = loudness * jnp.repeat(jnp.exp(heights), extent[position] // shards_of).reshape((-1,) + (1,) * (len(extent) - 1 - position))
    return loudness


def assign_block(rng, own, number, rows, count, top, limit, skew):
    ranking = jax.random.permutation(rng, count)
    crowded, ordinary = load_shares(count, rows * top, limit, skew, True), load_shares(count, rows * top, limit, skew, False)
    places = jnp.arange(count)

    def named(lengths, offset_by):
        used = int((lengths > 0).sum())
        fixed = max(1, used // 4)
        shifted = fixed + (places - fixed + offset_by * (used - fixed)) % max(1, count - fixed)
        return jnp.zeros((count,), jnp.int32).at[ranking[jnp.where(places < fixed, places, shifted)]].set(jnp.asarray(lengths, jnp.int32))

    lengths = jnp.where(number % 4 == 0, named(crowded, number // 4), named(ordinary, number - number // 4 - 1))
    mixed = jax.random.permutation(jax.random.fold_in(own, 3), count)
    source_of, sink = mixed[0:count // 2 * 2:2], mixed[1:count // 2 * 2:2]
    room = jnp.minimum(lengths[source_of] - 1, limit - lengths[sink]) // 2
    room = jnp.where((source_of == ranking[0]) | (sink == ranking[0]) | (lengths[sink] == 0), 0, jnp.maximum(room, 0))
    shifted = jax.random.randint(jax.random.fold_in(own, 4), (count // 2,), 0, 1 << 20) % (room + 1)
    lengths = lengths.at[source_of].add(-shifted).at[sink].add(shifted)
    members = jnp.searchsorted(jnp.cumsum(lengths), jnp.arange(rows * top), side="right").astype(jnp.int32)
    table = members.reshape(top, rows).T
    table = table[jax.random.permutation(jax.random.fold_in(own, 1), rows)]
    offset_by = jax.random.randint(jax.random.fold_in(own, 2), (rows, 1), 0, top)
    return jnp.take_along_axis(table, (jnp.arange(top)[None, :] + offset_by) % top, axis=1)


def load_shares(amount, total, most, lean, full):
    portions = [(1 << 20) // math.isqrt(grade ** lean) + 1 for grade in range(1, amount + 1)]
    largest = most if full else min(most, max(-(-total // amount), total * portions[0] // sum(portions)))
    least = 1 if total - largest >= amount - 1 else 0
    given, spare = [largest] + [least] * (amount - 1), total - largest - least * (amount - 1)
    while spare > 0:
        candidates = [i for i in range(1, amount) if given[i] < largest] or [i for i in range(1, amount) if given[i] < most]
        pool, remaining = sum([portions[i] for i in candidates]), spare
        for i in candidates:
            more = min(most - given[i], max(1, remaining * portions[i] // pool), spare)
            given[i] = given[i] + more
            spare = spare - more
    return np.array(given)


def centred(key, shape, deviation, reach, cuts=(), kind=jnp.bfloat16):
    array = deviation * jax.random.normal(key, shape, jnp.float32)
    if cuts:
        array = array * shard_levels(key, shape, cuts, -0.22, 0.18)
    return jnp.clip(array, -reach, reach).astype(kind)


def setup_inputs(seed: int = 0) -> dict:
    key_of = jax.random.split(jax.random.key(seed), 14)
    block_input = centred(key_of[0], (TOKENS, D), 1.0, 6.0, ((0, 8), (1, 4)), jnp.float32)
    ln1_gain = jnp.clip(1.0 + 0.15 * jax.random.normal(key_of[1], (D,), jnp.float32), 0.25, 1.75)
    ln1_bias = centred(key_of[2], (D,), 0.5, 3.0, ((0, 4),), jnp.float32)
    qkv_weight = centred(key_of[3], (D, 3 * D), D ** -0.5, 0.21875, ((0, 2), (1, 4)))
    out_weight = centred(key_of[4], (D, D), (D // 64) ** -0.5, 1.75, ((0, 2), (1, 4)))
    ln2_gain = jnp.clip(1.0 + 0.15 * jax.random.normal(key_of[5], (D,), jnp.float32), 0.25, 1.75)
    ln2_bias = centred(key_of[6], (D,), 0.5, 3.0, ((0, 4),), jnp.float32)
    router_weight = centred(key_of[7], (D, E), (2 * D) ** -0.5, 0.15625, ((0, 4),))
    expert_in = centred(key_of[8], (E, D, FF), D ** -0.5, 0.21875, ((0, 2), (2, 4)))
    expert_out = centred(key_of[9], (E, FF, D), (max(FF // 128, 1)) ** -0.5, 1.25, ((0, 2), (1, 4)))
    expert_ids_keys = jax.random.split(jax.random.fold_in(key_of[10], 1), TOKENS // (IMG_DEV * SEQ))
    expert_ids_turns = jax.random.permutation(jax.random.fold_in(key_of[10], 3), TOKENS // (IMG_DEV * SEQ))
    expert_ids = jax.vmap(lambda own, number: assign_block(jax.random.fold_in(key_of[10], 2), own, number, IMG_DEV * SEQ, E, 2, CAP, 1))(expert_ids_keys, expert_ids_turns).reshape((TOKENS, 2))
    kept_flags = with_ends((jax.random.randint(key_of[11], (TOKENS, 2), 0, 8) < 7).astype(jnp.int32), jax.random.fold_in(key_of[11], 1), 0, 1)
    cotangent = centred(key_of[12], (TOKENS, D), 1.0, 6.0, ((0, 8), (1, 4)), jnp.float32)
    return dict(block_input=block_input, ln1_gain=ln1_gain, ln1_bias=ln1_bias, qkv_weight=qkv_weight, out_weight=out_weight, ln2_gain=ln2_gain, ln2_bias=ln2_bias, router_weight=router_weight, expert_in=expert_in, expert_out=expert_out, expert_ids=expert_ids, kept_flags=kept_flags, cotangent=cotangent)


EPSILON = 1e-06
HIGHEST = lax.Precision.HIGHEST

@jax.custom_vjp
def low(v):
    return lax.optimization_barrier(v.astype(jnp.bfloat16)).astype(jnp.float32)

@jax.custom_vjp
def low_back(v):
    return v

def low_keep(v):
    return (low(v), None)

def low_pass(kept, grad):
    return (grad,)

def back_keep(v):
    return (v, None)

def back_low(kept, grad):
    return (low(grad),)
low.defvjp(low_keep, low_pass)
low_back.defvjp(back_keep, back_low)

def layer_norm(values, gain_vec, bias_vec):
    average = lax.optimization_barrier(jnp.mean(values, axis=1, keepdims=True))
    centered = values - average
    variance = lax.optimization_barrier(jnp.mean(centered * centered, axis=1, keepdims=True))
    return centered * lax.rsqrt(variance + EPSILON) * gain_vec + bias_vec

def route_tables(expert_ids):
    blocks = expert_ids.shape[0] // (IMG_DEV * SEQ)
    flat_ids = expert_ids.reshape(blocks, -1)
    one_hot = (flat_ids[:, :, None] == jnp.arange(E, dtype=jnp.int32)).astype(jnp.int32)
    slot_index = lax.optimization_barrier(jnp.sum(jnp.cumsum(one_hot, axis=1) * one_hot, axis=2)) - 1
    target = ((jnp.arange(blocks, dtype=jnp.int32)[:, None] * E + flat_ids) * CAP + slot_index).reshape(-1).astype(jnp.int32)
    route_total = target.shape[0]
    owners = jnp.full((blocks * E * CAP,), route_total, jnp.int32).at[target].set(jnp.arange(route_total, dtype=jnp.int32))
    return (target, owners, blocks)

def attend_group(qkv_group):
    queries = qkv_group[:, :, :, 0]
    key_vecs = qkv_group[:, :, :, 1]
    value_vecs = qkv_group[:, :, :, 2]
    scores = low_back(jnp.einsum('bqhd,bkhd->bhqk', queries, key_vecs, precision=HIGHEST) * (1.0 / math.sqrt(HEAD_DIM)))
    att_probs = jax.nn.softmax(scores, axis=-1)
    return jnp.einsum('bhqk,bkhd->bqhd', low(att_probs), value_vecs, precision=HIGHEST)

def forward(target, owners, blocks, kept_vals, expert_ids, block_input, ln1_gain, ln1_bias, qkv_weight, out_weight, ln2_gain, ln2_bias, router_weight, expert_in, expert_out):
    token_count = block_input.shape[0]
    h_one = low(layer_norm(block_input, ln1_gain, ln1_bias))
    qkv_vals = low_back(low(jnp.dot(h_one, qkv_weight, precision=HIGHEST)))
    groups = qkv_vals.reshape(-1, IMG_DEV, SEQ, HEADS, 3, HEAD_DIM)
    attended = lax.map(jax.checkpoint(attend_group), groups).reshape(token_count, HEADS * HEAD_DIM)
    attended = low_back(low(attended))
    mid = block_input + low_back(jnp.dot(attended, out_weight.T, precision=HIGHEST))
    h_two = low(layer_norm(mid, ln2_gain, ln2_bias))
    logits = low_back(jnp.dot(h_two, router_weight, precision=HIGHEST))
    route_probs = jax.nn.softmax(logits, axis=-1)
    choose = expert_ids[:, :, None] == jnp.arange(E, dtype=jnp.int32)
    gate_vals = lax.optimization_barrier(jnp.sum(jnp.where(choose, route_probs[:, None, :], 0.0), axis=2)) * kept_vals
    padded = jnp.concatenate([h_two, jnp.zeros((1, h_two.shape[1]), h_two.dtype)], axis=0)
    per_expert = jnp.transpose((owners // 2).reshape(blocks, E, CAP), (1, 0, 2)).reshape(E, -1)

    def one_expert(packed):
        index_rows, first_weight, second_weight = packed
        rows_in = low_back(padded[index_rows])
        hidden_pre = low_back(jnp.dot(rows_in, first_weight, precision=HIGHEST))
        hidden_act = low(jax.nn.gelu(hidden_pre, approximate=False))
        return low_back(low(jnp.dot(hidden_act, second_weight, precision=HIGHEST)))
    results = lax.map(jax.checkpoint(one_expert), (per_expert, expert_in, expert_out))
    flat_out = jnp.transpose(results.reshape(E, blocks, CAP, -1), (1, 0, 2, 3)).reshape(blocks * E * CAP, -1)
    routed = flat_out[target].reshape(token_count, 2, -1)
    return mid + lax.optimization_barrier(jnp.sum(routed * gate_vals[:, :, None], axis=1))

def reference(block_input, ln1_gain, ln1_bias, qkv_weight, out_weight, ln2_gain, ln2_bias, router_weight, expert_in, expert_out, expert_ids, kept_flags, cotangent):
    target, owners, blocks = route_tables(expert_ids)
    floats = [item.astype(jnp.float32) for item in (block_input, ln1_gain, ln1_bias, qkv_weight, out_weight, ln2_gain, ln2_bias, router_weight, expert_in, expert_out)]
    kept_vals = kept_flags.astype(jnp.float32)
    output, pullback = jax.vjp(partial(forward, target, owners, blocks, kept_vals, expert_ids), *floats)
    grads = pullback(cotangent.astype(jnp.float32))
    return (output, grads[0], grads[3], grads[4], grads[7], grads[8], grads[9], grads[1], grads[2], grads[5], grads[6])
```

```python
from functools import partial
import math

import jax
import jax.numpy as jnp
from jax import lax
from jax.sharding import PartitionSpec as P

HEAD_DIM = 64
E = 32
SEQ = 197
CAP = 168
PARTS = 4
SIDE = 128

EPSILON = 1e-06
F32 = jnp.float32
LOW = jnp.bfloat16
CONTRACT_ROWS = (((0,), (0,)), ((), ()))
CONTRACT_COLS = (((1,), (1,)), ((), ()))


def over_rows(left, right):
    return lax.dot_general(left, right, CONTRACT_ROWS, preferred_element_type=F32)


def over_cols(left, right):
    return lax.dot_general(left, right, CONTRACT_COLS, preferred_element_type=F32)


def matmul(left, right):
    return jnp.dot(left, right, preferred_element_type=F32)


def col_gather(values):
    return lax.all_gather(values, "col", axis=1, tiled=True)


def col_scatter(values):
    return lax.psum_scatter(values, "col", scatter_dimension=1, tiled=True)


def row_swap(values):
    return lax.ppermute(values, "row", ((0, 1), (1, 0)))


def row_gather(values):
    if lax.axis_size("row") == 2:
        return jnp.stack((values, row_swap(values)))
    return lax.all_gather(values, "row", axis=0)


def row_reduce(stacked):
    if lax.axis_size("row") == 2:
        return stacked[0].astype(F32) + row_swap(stacked[1]).astype(F32)
    return lax.psum_scatter(stacked, "row", scatter_dimension=0).astype(F32)


def own_block(stacked):
    if lax.axis_size("row") == 2:
        return stacked[0]
    return lax.dynamic_index_in_dim(stacked, lax.axis_index("row"), 0, keepdims=False)


def own_cols(values, width):
    return lax.dynamic_slice_in_dim(values, lax.axis_index("col") * width, width, values.ndim - 1)


def statistics(values):
    average = jnp.mean(values, axis=-1, keepdims=True)
    centered = values - average
    return average, lax.rsqrt(jnp.mean(centered * centered, axis=-1, keepdims=True) + EPSILON)


def split_low(values):
    head = values.astype(LOW)
    return head, (values - head.astype(F32)).astype(LOW)


def replica_sum(into, grad, start):
    count = lax.axis_size("dp")
    experts = grad.shape[0]
    if count != 4:
        total = lax.psum(grad, "dp").astype(F32)
        return lax.dynamic_update_slice_in_dim(into, total, start, 0)
    core = lax.axis_index("dp") % 2
    flat = grad.reshape(experts * 2, grad.shape[1] // 2, grad.shape[2])
    mine = lax.dynamic_slice_in_dim(flat, core * experts, experts, 0)
    theirs = lax.dynamic_slice_in_dim(flat, (1 - core) * experts, experts, 0)
    beside = ((0, 1), (1, 0), (2, 3), (3, 2))
    across = ((0, 2), (2, 0), (1, 3), (3, 1))
    pair = (mine.astype(F32) + lax.ppermute(theirs, "dp", beside).astype(F32)).astype(LOW)
    total = (pair.astype(F32) + lax.ppermute(pair, "dp", across).astype(F32)).astype(LOW)
    other = lax.ppermute(total, "dp", beside)
    into = lax.dynamic_update_slice_in_dim(into, total.astype(F32), 2 * start + core * experts, 0)
    return lax.dynamic_update_slice_in_dim(
        into, other.astype(F32), 2 * start + (1 - core) * experts, 0
    )


def body(
    block_input,
    ln1_gain,
    ln1_bias,
    qkv_weight,
    out_weight,
    ln2_gain,
    ln2_bias,
    router_weight,
    expert_in,
    expert_out,
    expert_ids,
    kept_flags,
    cotangent,
):
    tokens_here, col_width = block_input.shape
    full_width = col_width * lax.axis_size("col")
    row_count = lax.axis_size("row")
    local_experts = expert_in.shape[0]
    images = tokens_here // SEQ
    score_scale = 1.0 / math.sqrt(HEAD_DIM)

    x_full = col_gather(block_input.astype(LOW))
    vectors = col_gather(jnp.stack((ln1_gain, ln1_bias, ln2_gain, ln2_bias)))
    gain_one, bias_one, gain_two, bias_two = vectors
    qkv_full = lax.all_gather(qkv_weight, "row", axis=0, tiled=True)
    proj_mine = lax.all_gather(out_weight, "row", axis=0, tiled=True)

    average_one, inv_one = statistics(x_full.astype(F32))
    h_one_full = ((x_full.astype(F32) - average_one) * inv_one * gain_one + bias_one).astype(LOW)
    scaled_one = (block_input - average_one) * inv_one

    routes = row_gather(jnp.concatenate((expert_ids, kept_flags), axis=1))
    ids_all, kept_all = routes[:, :, :2], routes[:, :, 2:].reshape(-1, 2).astype(F32)
    expert_range = jnp.arange(E, dtype=jnp.int32)
    flat_ids = ids_all.reshape(row_count, -1)
    one_hot = (flat_ids[:, :, None] == expert_range).astype(jnp.int32)
    slot_index = jnp.sum(jnp.cumsum(one_hot, axis=1) * one_hot, axis=2) - 1
    local_id = flat_ids - lax.axis_index("row") * local_experts
    source = jnp.arange(row_count, dtype=jnp.int32)[:, None]
    slot_total = local_experts * row_count * CAP
    target = (local_id * row_count + source) * CAP + slot_index
    is_here = (local_id >= 0) & (local_id < local_experts)
    target = jnp.where(is_here, target, slot_total).reshape(-1)
    route_total = target.shape[0]
    all_tokens = route_total // 2
    owners = (
        jnp.full((slot_total,), route_total, jnp.int32)
        .at[target]
        .set(jnp.arange(route_total, dtype=jnp.int32), mode="drop")
    )
    slot_used = owners < route_total
    slot_token = jnp.minimum(owners // 2, all_tokens - 1)

    qkv_vals = matmul(h_one_full, qkv_full).astype(LOW)
    heads_here = qkv_vals.shape[1] // (3 * HEAD_DIM)
    qkv_grid = qkv_vals.reshape(images, SEQ, heads_here, 3, HEAD_DIM)
    queries = qkv_grid[:, :, :, 0]
    key_vecs = qkv_grid[:, :, :, 1]
    value_vecs = qkv_grid[:, :, :, 2]
    scores = (
        jnp.einsum("bqhd,bkhd->bhqk", queries, key_vecs, preferred_element_type=F32) * score_scale
    )
    largest = jnp.max(scores, axis=-1, keepdims=True)
    log_total = largest + jnp.log(jnp.sum(jnp.exp(scores - largest), axis=-1, keepdims=True))
    probs_low = jnp.exp(scores - log_total).astype(LOW)
    attended = jnp.einsum("bhqk,bkhd->bqhd", probs_low, value_vecs, preferred_element_type=F32)
    attended = attended.reshape(tokens_here, heads_here * HEAD_DIM).astype(LOW)

    cotangent_low, x_own, proj_late, router_late = lax.optimization_barrier(
        (cotangent.astype(LOW), x_full, proj_mine, router_weight)
    )
    cot_full = col_gather(cotangent_low)
    proj_full = col_gather(proj_late)
    router_full = lax.all_gather(router_late, "col", axis=0, tiled=True)
    x_all = row_gather(x_own).reshape(all_tokens, full_width)
    cot_all = row_gather(cot_full).reshape(all_tokens, full_width)
    cot_rows = jnp.take(cot_all, slot_token, axis=0, mode="clip").reshape(
        local_experts, row_count * CAP, full_width
    )

    attended_full = col_gather(attended)
    attended_all = row_gather(attended_full).reshape(all_tokens, full_width)
    mid_all = x_all.astype(F32) + over_cols(attended_all, proj_full)
    proj_cols = lax.dynamic_slice_in_dim(
        proj_full, lax.axis_index("col") * col_width, col_width, 0
    )
    mid = block_input + over_cols(attended_full, proj_cols)
    average_two, inv_two = statistics(mid_all)
    scaled_two = (mid_all - average_two) * inv_two
    h_two = (scaled_two * gain_two + bias_two).astype(LOW)
    route_probs = jax.nn.softmax(matmul(h_two, router_full), axis=-1)
    ids_flat = ids_all.reshape(-1, 2)
    choose = ids_flat[:, :, None] == expert_range
    kept_choose = jnp.sum(jnp.where(choose, kept_all[:, :, None], 0.0), axis=1)
    gate_head, gate_tail = split_low(route_probs * kept_choose)
    side = jnp.concatenate(
        (gate_head, gate_tail, jnp.zeros((all_tokens, SIDE - 2 * E), LOW)), axis=1
    )
    table = jnp.concatenate((h_two, side), axis=1)

    slot_token = slot_token.reshape(local_experts, -1)
    slot_used = slot_used.reshape(local_experts, -1)
    step = max(1, local_experts // PARTS)
    my_experts = lax.axis_index("row") * local_experts + jnp.arange(local_experts)
    results, backs, grads = [], [], []
    for start in range(0, local_experts, step):
        part = slice(start, start + step)
        weight_in, weight_out = expert_in[part], expert_out[part]
        fetched = jnp.take(table, slot_token[part].reshape(-1), axis=0, mode="clip").reshape(
            step, row_count * CAP, -1
        )
        rows_in = fetched[:, :, :full_width]
        gate_cols = fetched[:, :, full_width:].astype(F32)
        named = (my_experts[part, None] == expert_range)[:, None, :]
        gate = jnp.sum(
            jnp.where(named, gate_cols[:, :, :E] + gate_cols[:, :, E : 2 * E], 0.0),
            axis=2,
            keepdims=True,
        )
        gate = jnp.where(slot_used[part][:, :, None], gate, 0.0)
        cot_part = cot_rows[part]
        pre = jnp.einsum("ecd,edf->ecf", rows_in, weight_in, preferred_element_type=F32)
        phi = 0.5 * (1.0 + lax.erf(pre * math.sqrt(0.5)))
        act = pre * phi
        slope = phi + pre * (jnp.exp(-0.5 * pre * pre) * (1.0 / math.sqrt(2.0 * math.pi)))
        back = jnp.einsum("ecd,efd->ecf", cot_part, weight_out, preferred_element_type=F32)
        gate_back = jnp.sum(act * back, axis=2, keepdims=True)
        pre_grad = (gate * back * slope).astype(LOW)
        act_gated = (gate * act).astype(LOW)
        input_part = jnp.einsum("ecf,edf->ecd", pre_grad, weight_in, preferred_element_type=F32)
        back_head, back_tail = split_low(gate_back)
        backs.append(
            jnp.concatenate(
                (
                    input_part.astype(LOW),
                    back_head,
                    back_tail,
                    jnp.zeros(gate_back.shape[:2] + (SIDE - 2,), LOW),
                ),
                axis=2,
            ).reshape(-1, full_width + SIDE)
        )
        results.append(
            jnp.einsum("ecf,efd->ecd", act_gated, weight_out, preferred_element_type=F32)
            .astype(LOW)
            .reshape(-1, full_width)
        )
        grads.append(
            (
                jnp.einsum("ecd,ecf->edf", rows_in, pre_grad, preferred_element_type=F32),
                jnp.einsum("ecf,ecd->efd", act_gated, cot_part, preferred_element_type=F32),
            )
        )
    expert_in_sum = jnp.zeros(expert_in.shape, F32)
    expert_out_sum = jnp.zeros(expert_out.shape, F32)
    if lax.axis_size("dp") == 4:
        expert_in_sum = expert_in_sum.reshape(2 * local_experts, full_width // 2, -1)
        expert_out_sum = expert_out_sum.reshape(2 * local_experts, expert_out.shape[1] // 2, -1)
    for place, (grad_in, grad_out) in enumerate(grads):
        expert_in_sum = replica_sum(expert_in_sum, grad_in.astype(LOW), place * step)
        expert_out_sum = replica_sum(expert_out_sum, grad_out.astype(LOW), place * step)
    expert_in_sum = expert_in_sum.reshape(expert_in.shape)
    expert_out_sum = expert_out_sum.reshape(expert_out.shape)

    back_rows = jnp.take(
        jnp.concatenate(backs), target, axis=0, mode="fill", fill_value=0
    ).reshape(all_tokens, 2, full_width + SIDE)
    back_sum = jnp.sum(back_rows[:, :, :full_width].astype(F32), axis=1)
    gate_grad = (
        back_rows[:, :, full_width].astype(F32) + back_rows[:, :, full_width + 1].astype(F32)
    ) * kept_all
    prob_grad = jnp.sum(jnp.where(choose, gate_grad[:, :, None], 0.0), axis=1)
    logit_grad = (
        route_probs * (prob_grad - jnp.sum(route_probs * prob_grad, axis=1, keepdims=True))
    ).astype(LOW)
    grad_router = over_rows(h_two, logit_grad)
    h_two_part = (back_sum + over_cols(logit_grad, router_full)).astype(LOW)
    h_two_sum = col_scatter(
        row_reduce(h_two_part.reshape(row_count, tokens_here, full_width)).astype(LOW)
    )
    h_two_grad = col_gather(h_two_sum).astype(F32)

    result_rows = jnp.take(
        jnp.concatenate(results), target, axis=0, mode="fill", fill_value=0
    ).reshape(row_count, tokens_here, 2, full_width)
    result_part = jnp.sum(result_rows.astype(F32), axis=2).astype(LOW)
    output = mid + col_scatter(row_reduce(result_part).astype(LOW)).astype(F32)

    scaled_own = own_block(scaled_two.reshape(row_count, tokens_here, full_width))
    inv_own = own_block(inv_two.reshape(row_count, tokens_here, 1))
    grad_two = h_two_grad * gain_two
    norm_two_grad = inv_own * (
        grad_two
        - jnp.mean(grad_two, axis=1, keepdims=True)
        - scaled_own * jnp.mean(grad_two * scaled_own, axis=1, keepdims=True)
    )
    ln2_gain_grad = own_cols(jnp.sum(h_two_grad * scaled_own, axis=0), col_width)
    ln2_bias_grad = own_cols(jnp.sum(h_two_grad, axis=0), col_width)
    mid_full = (cot_full.astype(F32) + norm_two_grad).astype(LOW)
    mid_grad = cotangent + own_cols(norm_two_grad, col_width)

    grad_proj = over_rows(mid_full, attended)
    att_grad = matmul(mid_full, proj_mine).astype(LOW)
    att_grad = att_grad.reshape(images, SEQ, heads_here, HEAD_DIM)
    scores_again = (
        jnp.einsum("bqhd,bkhd->bhqk", queries, key_vecs, preferred_element_type=F32) * score_scale
    )
    att_probs = jnp.exp(scores_again - log_total)
    prob_grads = jnp.einsum("bqhd,bkhd->bhqk", att_grad, value_vecs, preferred_element_type=F32)
    score_grad = (
        att_probs * (prob_grads - jnp.sum(att_probs * prob_grads, axis=-1, keepdims=True))
    ).astype(LOW)
    query_grad = (
        jnp.einsum("bhqk,bkhd->bqhd", score_grad, key_vecs, preferred_element_type=F32)
        * score_scale
    )
    key_grad = (
        jnp.einsum("bhqk,bqhd->bkhd", score_grad, queries, preferred_element_type=F32)
        * score_scale
    )
    value_grad = jnp.einsum(
        "bhqk,bqhd->bkhd", att_probs.astype(LOW), att_grad, preferred_element_type=F32
    )
    qkv_grad = (
        jnp.stack((query_grad, key_grad, value_grad), axis=3).reshape(tokens_here, -1).astype(LOW)
    )
    h_one_part = over_cols(qkv_grad, qkv_full)
    h_one_grad = col_scatter(h_one_part.astype(LOW)).astype(F32)
    grad_qkv = over_rows(h_one_full, qkv_grad)

    scaled_full = (x_full.astype(F32) - average_one) * inv_one
    grad_one_part = h_one_part * gain_one
    sums = lax.psum(
        jnp.stack((jnp.sum(grad_one_part, axis=1), jnp.sum(grad_one_part * scaled_full, axis=1))),
        "col",
    )
    grad_one = h_one_grad * ln1_gain
    norm_one_grad = inv_one * (
        grad_one
        - sums[0][:, None] / full_width
        - scaled_one * (sums[1][:, None] / full_width)
    )
    grad_input = mid_grad + norm_one_grad
    ln1_gain_grad = jnp.sum(h_one_grad * scaled_one, axis=0)
    ln1_bias_grad = jnp.sum(h_one_grad, axis=0)

    router_sum = lax.dynamic_slice_in_dim(
        lax.psum(grad_router, ("dp", "row", "col")), lax.axis_index("col") * col_width, col_width, 0
    )
    weights_sum = lax.psum(
        lax.psum_scatter(
            jnp.concatenate((grad_qkv, grad_proj), axis=1), "row", scatter_dimension=0, tiled=True
        ),
        "dp",
    )
    qkv_sum = weights_sum[:, : qkv_weight.shape[1]]
    proj_sum = weights_sum[:, qkv_weight.shape[1] :]
    vector_sums = lax.psum(
        jnp.stack((ln1_gain_grad, ln1_bias_grad, ln2_gain_grad, ln2_bias_grad)), ("dp", "row")
    )
    return (
        output,
        grad_input,
        qkv_sum,
        proj_sum,
        router_sum,
        expert_in_sum,
        expert_out_sum,
        vector_sums[0],
        vector_sums[1],
        vector_sums[2],
        vector_sums[3],
    )


def col_stats(summed, squares):
    return lax.psum((summed, squares), "col")


def col_total(values):
    return lax.psum(values, "col")


def routed_swap(values):
    return lax.all_to_all(values, "row", split_axis=0, concat_axis=0, tiled=True)


def normalize(values, gain_vec, bias_vec, full_width):
    summed, squares = col_stats(jnp.sum(values, axis=1), jnp.sum(values * values, axis=1))
    average = summed / full_width
    inv_std = lax.rsqrt(squares / full_width - average * average + EPSILON)
    scaled = (values - average[:, None]) * inv_std[:, None]
    return (scaled, inv_std, scaled * gain_vec + bias_vec)


def normalize_back(grad_out, scaled, inv_std, gain_vec, full_width):
    scaled_grad = grad_out * gain_vec
    summed, crossed = col_stats(jnp.sum(scaled_grad, axis=1), jnp.sum(scaled_grad * scaled, axis=1))
    grad_in = inv_std[:, None] * (
        scaled_grad - summed[:, None] / full_width - scaled * (crossed[:, None] / full_width)
    )
    return (grad_in, jnp.sum(grad_out * scaled, axis=0), jnp.sum(grad_out, axis=0))


def exchange_body(
    block_input,
    ln1_gain,
    ln1_bias,
    qkv_weight,
    out_weight,
    ln2_gain,
    ln2_bias,
    router_weight,
    expert_in,
    expert_out,
    expert_ids,
    kept_flags,
    cotangent,
):
    tokens_here, col_width = block_input.shape
    full_width = col_width * lax.axis_size("col")
    row_count = lax.axis_size("row")
    local_experts = expert_in.shape[0]
    images = tokens_here // SEQ
    score_scale = 1.0 / math.sqrt(HEAD_DIM)
    scaled_one, inv_one, normed_one = normalize(block_input, ln1_gain, ln1_bias, full_width)
    h_one_full = col_gather(normed_one.astype(jnp.bfloat16))
    qkv_full, proj_full = (
        lax.all_gather(qkv_weight, "row", axis=0, tiled=True),
        lax.all_gather(out_weight, "row", axis=0, tiled=True),
    )
    qkv_vals = jnp.dot(h_one_full, qkv_full, preferred_element_type=jnp.float32).astype(
        jnp.bfloat16
    )
    heads_here = qkv_vals.shape[1] // (3 * HEAD_DIM)
    qkv_grid = qkv_vals.reshape(images, SEQ, heads_here, 3, HEAD_DIM)
    queries = qkv_grid[:, :, :, 0]
    key_vecs = qkv_grid[:, :, :, 1]
    value_vecs = qkv_grid[:, :, :, 2]
    scores = (
        jnp.einsum("bqhd,bkhd->bhqk", queries, key_vecs, preferred_element_type=jnp.float32)
        * score_scale
    )
    largest = jnp.max(scores, axis=-1, keepdims=True)
    log_total = largest + jnp.log(jnp.sum(jnp.exp(scores - largest), axis=-1, keepdims=True))
    probs_low = jnp.exp(scores - log_total).astype(jnp.bfloat16)
    attended = jnp.einsum(
        "bhqk,bkhd->bqhd", probs_low, value_vecs, preferred_element_type=jnp.float32
    )
    attended = attended.reshape(tokens_here, heads_here * HEAD_DIM).astype(jnp.bfloat16)
    mid = block_input + col_scatter(over_cols(attended, proj_full))
    scaled_two, inv_two, normed_two = normalize(mid, ln2_gain, ln2_bias, full_width)
    h_two = normed_two.astype(jnp.bfloat16)
    logits = col_total(jnp.dot(h_two, router_weight, preferred_element_type=jnp.float32))
    route_probs = jax.nn.softmax(logits, axis=-1)
    expert_range = jnp.arange(E, dtype=jnp.int32)
    choose = expert_ids[:, :, None] == expert_range
    kept_vals = kept_flags.astype(jnp.float32)
    gate_vals = jnp.sum(jnp.where(choose, route_probs[:, None, :], 0.0), axis=2) * kept_vals
    flat_ids = expert_ids.reshape(-1)
    one_hot = (flat_ids[:, None] == expert_range).astype(jnp.int32)
    slot_index = jnp.sum(jnp.cumsum(one_hot, axis=0) * one_hot, axis=1) - 1
    target = flat_ids * CAP + slot_index
    route_total = flat_ids.shape[0]
    owners = (
        jnp.full((E * CAP,), route_total, jnp.int32)
        .at[target]
        .set(jnp.arange(route_total, dtype=jnp.int32))
    )
    dispatch = jnp.take(h_two, owners // 2, axis=0, mode="fill", fill_value=0)
    arrived = routed_swap(dispatch.reshape(row_count, -1, col_width))
    rows_in = col_gather(arrived.reshape(-1, col_width)).reshape(
        row_count, local_experts, CAP, full_width
    )
    first_full, second_full = (expert_in, expert_out)
    hidden_pre = jnp.einsum(
        "secd,edf->secf", rows_in, first_full, preferred_element_type=jnp.float32
    )
    hidden_act = jax.nn.gelu(hidden_pre, approximate=False).astype(jnp.bfloat16)
    expert_part = jnp.einsum(
        "secf,efd->secd", hidden_act, second_full, preferred_element_type=jnp.float32
    )
    returned = col_scatter(expert_part.reshape(-1, full_width)).astype(jnp.bfloat16)
    results = routed_swap(returned.reshape(row_count, -1, col_width)).reshape(E * CAP, col_width)
    routed = (
        jnp.take(results, target, axis=0).reshape(tokens_here, 2, col_width).astype(jnp.float32)
    )
    output = mid + jnp.sum(routed * gate_vals[:, :, None], axis=1)
    gate_grad = col_total(jnp.sum(cotangent[:, None, :] * routed, axis=2)) * kept_vals
    prob_grad = jnp.sum(jnp.where(choose, gate_grad[:, :, None], 0.0), axis=1)
    logit_grad = (
        route_probs * (prob_grad - jnp.sum(route_probs * prob_grad, axis=1, keepdims=True))
    ).astype(jnp.bfloat16)
    grad_router = over_rows(h_two, logit_grad)
    route_grad = (
        (cotangent[:, None, :] * gate_vals[:, :, None]).reshape(-1, col_width).astype(jnp.bfloat16)
    )
    grad_buffer = jnp.take(route_grad, owners, axis=0, mode="fill", fill_value=0)
    grad_arrived = routed_swap(grad_buffer.reshape(row_count, -1, col_width))
    grad_rows = col_gather(grad_arrived.reshape(-1, col_width)).reshape(
        row_count, local_experts, CAP, full_width
    )
    act_grad = jnp.einsum(
        "secd,efd->secf", grad_rows, second_full, preferred_element_type=jnp.float32
    )
    act_pullback = jax.vjp(partial(jax.nn.gelu, approximate=False), hidden_pre)[1]
    pre_grad = act_pullback(act_grad)[0].astype(jnp.bfloat16)
    grad_expert_out = jnp.einsum(
        "secf,secd->efd", hidden_act, grad_rows, preferred_element_type=jnp.float32
    )
    grad_expert_in = jnp.einsum(
        "secd,secf->edf", rows_in, pre_grad, preferred_element_type=jnp.float32
    )
    input_part = jnp.einsum(
        "secf,edf->secd", pre_grad, first_full, preferred_element_type=jnp.float32
    )
    grad_back = col_scatter(input_part.reshape(-1, full_width)).astype(jnp.bfloat16)
    grad_return = routed_swap(grad_back.reshape(row_count, -1, col_width)).reshape(
        E * CAP, col_width
    )
    grad_two_in = (
        jnp.take(grad_return, target, axis=0).reshape(tokens_here, 2, col_width).astype(jnp.float32)
    )
    h_two_grad = jnp.sum(grad_two_in, axis=1) + over_cols(logit_grad, router_weight)
    norm_two_grad, ln2_gain_grad, ln2_bias_grad = normalize_back(
        h_two_grad, scaled_two, inv_two, ln2_gain, full_width
    )
    mid_grad = cotangent + norm_two_grad
    mid_full = col_gather(mid_grad.astype(jnp.bfloat16))
    grad_proj = over_rows(mid_full, attended)
    att_grad = jnp.dot(mid_full, proj_full, preferred_element_type=jnp.float32).astype(jnp.bfloat16)
    att_grad = att_grad.reshape(images, SEQ, heads_here, HEAD_DIM)
    scores_again = (
        jnp.einsum("bqhd,bkhd->bhqk", queries, key_vecs, preferred_element_type=jnp.float32)
        * score_scale
    )
    att_probs = jnp.exp(scores_again - log_total)
    prob_grads = jnp.einsum(
        "bqhd,bkhd->bhqk", att_grad, value_vecs, preferred_element_type=jnp.float32
    )
    score_grad = (
        att_probs * (prob_grads - jnp.sum(att_probs * prob_grads, axis=-1, keepdims=True))
    ).astype(jnp.bfloat16)
    query_grad = (
        jnp.einsum("bhqk,bkhd->bqhd", score_grad, key_vecs, preferred_element_type=jnp.float32)
        * score_scale
    )
    key_grad = (
        jnp.einsum("bhqk,bqhd->bkhd", score_grad, queries, preferred_element_type=jnp.float32)
        * score_scale
    )
    value_grad = jnp.einsum(
        "bhqk,bqhd->bkhd",
        att_probs.astype(jnp.bfloat16),
        att_grad,
        preferred_element_type=jnp.float32,
    )
    qkv_grad = (
        jnp.stack((query_grad, key_grad, value_grad), axis=3)
        .reshape(tokens_here, -1)
        .astype(jnp.bfloat16)
    )
    grad_qkv = over_rows(h_one_full, qkv_grad)
    h_one_grad = col_scatter(over_cols(qkv_grad, qkv_full))
    norm_one_grad, ln1_gain_grad, ln1_bias_grad = normalize_back(
        h_one_grad, scaled_one, inv_one, ln1_gain, full_width
    )
    grad_input = mid_grad + norm_one_grad
    rows_here = qkv_weight.shape[0]
    totals_all = lax.psum(
        (
            grad_qkv,
            grad_proj,
            grad_router,
            ln1_gain_grad,
            ln1_bias_grad,
            ln2_gain_grad,
            ln2_bias_grad,
        ),
        ("dp", "row"),
    )
    row_start = lax.axis_index("row") * rows_here
    qkv_sum = lax.dynamic_slice_in_dim(totals_all[0], row_start, rows_here, 0)
    proj_sum = lax.dynamic_slice_in_dim(totals_all[1], row_start, rows_here, 0)
    router_sum = totals_all[2]
    gain_one = totals_all[3]
    bias_one = totals_all[4]
    gain_two = totals_all[5]
    bias_two = totals_all[6]
    expert_in_sum, expert_out_sum = lax.psum((grad_expert_in, grad_expert_out), "dp")
    return (
        output,
        grad_input,
        qkv_sum,
        proj_sum,
        router_sum,
        expert_in_sum,
        expert_out_sum,
        gain_one,
        bias_one,
        gain_two,
        bias_two,
    )


def solution(mesh):
    in_specs = (
        P(("dp", "row"), "col"),
        P("col"),
        P("col"),
        P("row", "col"),
        P("row", "col"),
        P("col"),
        P("col"),
        P("col", None),
        P("row", None, "col"),
        P("row", "col", None),
        P(("dp", "row"), None),
        P(("dp", "row"), None),
        P(("dp", "row"), "col"),
    )
    out_specs = (
        P(("dp", "row"), "col"),
        P(("dp", "row"), "col"),
        P("row", "col"),
        P("row", "col"),
        P("col", None),
        P("row", None, "col"),
        P("row", "col", None),
        P("col"),
        P("col"),
        P("col"),
        P("col"),
    )
    chosen = body if mesh.shape["row"] == 2 else exchange_body
    return jax.shard_map(chosen, mesh=mesh, in_specs=in_specs, out_specs=out_specs, check_vma=False)
```

```python
from functools import partial
import math

import jax
import jax.numpy as jnp
from jax import lax
from jax.sharding import PartitionSpec as P

HEAD_DIM = 64
E = 32
SEQ = 197
CAP = 168
PARTS = 4
SIDE = 128

EPSILON = 1e-06
F32 = jnp.float32
LOW = jnp.bfloat16
CONTRACT_ROWS = (((0,), (0,)), ((), ()))
CONTRACT_COLS = (((1,), (1,)), ((), ()))


def over_rows(left, right):
    return lax.dot_general(left, right, CONTRACT_ROWS, preferred_element_type=F32)


def over_cols(left, right):
    return lax.dot_general(left, right, CONTRACT_COLS, preferred_element_type=F32)


def matmul(left, right):
    return jnp.dot(left, right, preferred_element_type=F32)


def col_gather(values):
    return lax.all_gather(values, "col", axis=1, tiled=True)


def col_scatter(values):
    return lax.psum_scatter(values, "col", scatter_dimension=1, tiled=True)


def row_swap(values):
    return lax.ppermute(values, "row", ((0, 1), (1, 0)))


def row_gather(values):
    return jnp.concatenate((values, row_swap(values)))


def row_reduce(values):
    here = values.shape[0] // 2
    return values[:here].astype(F32) + row_swap(values[here:]).astype(F32)


def pad_rows(values, rows, fill=0):
    extra = jnp.full((rows - values.shape[0],) + values.shape[1:], fill, values.dtype)
    return jnp.concatenate((values, extra))


def own_cols(values, width):
    return lax.dynamic_slice_in_dim(values, lax.axis_index("col") * width, width, values.ndim - 1)


def statistics(values):
    average = jnp.mean(values, axis=-1, keepdims=True)
    centered = values - average
    return average, lax.rsqrt(jnp.mean(centered * centered, axis=-1, keepdims=True) + EPSILON)


def split_low(values):
    head = values.astype(LOW)
    return head, (values - head.astype(F32)).astype(LOW)


BESIDE = ((0, 1), (1, 0), (2, 3), (3, 2))
ACROSS = ((0, 2), (2, 0), (1, 3), (3, 1))


def add_beside(grad):
    if lax.axis_size("dp") != 4:
        return grad
    experts = grad.shape[0]
    core = lax.axis_index("dp") % 2
    flat = grad.reshape(experts * 2, grad.shape[1] // 2, grad.shape[2])
    mine = lax.dynamic_slice_in_dim(flat, core * experts, experts, 0)
    theirs = lax.dynamic_slice_in_dim(flat, (1 - core) * experts, experts, 0)
    return (mine.astype(F32) + lax.ppermute(theirs, "dp", BESIDE).astype(F32)).astype(LOW)


def add_across(pair):
    if lax.axis_size("dp") != 4:
        return lax.psum(pair, "dp")
    return (pair.astype(F32) + lax.ppermute(pair, "dp", ACROSS).astype(F32)).astype(LOW)


def store_both(into, total, start):
    if lax.axis_size("dp") != 4:
        return lax.dynamic_update_slice_in_dim(into, total.astype(F32), start, 0)
    experts = total.shape[0]
    core = lax.axis_index("dp") % 2
    other = lax.ppermute(total, "dp", BESIDE)
    into = lax.dynamic_update_slice_in_dim(into, total.astype(F32), 2 * start + core * experts, 0)
    return lax.dynamic_update_slice_in_dim(
        into, other.astype(F32), 2 * start + (1 - core) * experts, 0
    )


def body(
    block_input,
    ln1_gain,
    ln1_bias,
    qkv_weight,
    out_weight,
    ln2_gain,
    ln2_bias,
    router_weight,
    expert_in,
    expert_out,
    expert_ids,
    kept_flags,
    cotangent,
):
    tokens_here, col_width = block_input.shape
    full_width = col_width * lax.axis_size("col")
    row_count = lax.axis_size("row")
    local_experts = expert_in.shape[0]
    images = tokens_here // SEQ
    score_scale = 1.0 / math.sqrt(HEAD_DIM)

    padded_tokens = -(-tokens_here // 16) * 16
    x_full = col_gather(pad_rows(block_input.astype(LOW), padded_tokens))
    vectors = col_gather(jnp.stack((ln1_gain, ln1_bias, ln2_gain, ln2_bias)))
    gain_one, bias_one, gain_two, bias_two = vectors
    qkv_full = lax.all_gather(qkv_weight, "row", axis=0, tiled=True)
    proj_mine = lax.all_gather(out_weight, "row", axis=0, tiled=True)

    ids_all = row_gather(pad_rows(expert_ids, padded_tokens, E))
    kept_all = row_gather(pad_rows(kept_flags, padded_tokens)).astype(F32)
    expert_range = jnp.arange(E, dtype=jnp.int32)
    flat_ids = ids_all.reshape(row_count, -1)
    one_hot = (flat_ids[:, :, None] == expert_range).astype(jnp.int32)
    slot_index = jnp.sum(jnp.cumsum(one_hot, axis=1) * one_hot, axis=2) - 1
    local_id = flat_ids - lax.axis_index("row") * local_experts
    source = jnp.arange(row_count, dtype=jnp.int32)[:, None]
    slot_total = local_experts * row_count * CAP
    target = (local_id * row_count + source) * CAP + slot_index
    is_here = (local_id >= 0) & (local_id < local_experts)
    target = jnp.where(is_here, target, slot_total).reshape(-1)
    route_total = target.shape[0]
    all_tokens = route_total // 2
    owners = (
        jnp.full((slot_total,), route_total, jnp.int32)
        .at[target]
        .set(jnp.arange(route_total, dtype=jnp.int32), mode="drop")
    )
    slot_used = owners < route_total
    slot_token = jnp.minimum(owners // 2, all_tokens - 1)
    if lax.axis_size("dp") == 4:
        expert_in_sum = jnp.zeros((2 * local_experts, expert_in.shape[1] // 2, expert_in.shape[2]), F32)
        expert_out_sum = jnp.zeros(
            (2 * local_experts, expert_out.shape[1] // 2, expert_out.shape[2]), F32
        )
    else:
        expert_in_sum = jnp.zeros(expert_in.shape, F32)
        expert_out_sum = jnp.zeros(expert_out.shape, F32)
    x_padded, slot_token, slot_used, target = lax.optimization_barrier(
        (x_full, slot_token, slot_used, target)
    )
    x_full = x_padded[:tokens_here]

    average_one, inv_one = statistics(x_full.astype(F32))
    h_one_full = ((x_full.astype(F32) - average_one) * inv_one * gain_one + bias_one).astype(LOW)
    scaled_one = (block_input - average_one) * inv_one

    qkv_vals = matmul(h_one_full, qkv_full).astype(LOW)
    heads_here = qkv_vals.shape[1] // (3 * HEAD_DIM)
    qkv_grid = qkv_vals.reshape(images, SEQ, heads_here, 3, HEAD_DIM)
    queries = qkv_grid[:, :, :, 0]
    key_vecs = qkv_grid[:, :, :, 1]
    value_vecs = qkv_grid[:, :, :, 2]
    scores = (
        jnp.einsum("bqhd,bkhd->bhqk", queries, key_vecs, preferred_element_type=F32) * score_scale
    )
    largest = jnp.max(scores, axis=-1, keepdims=True)
    log_total = largest + jnp.log(jnp.sum(jnp.exp(scores - largest), axis=-1, keepdims=True))
    probs_low = jnp.exp(scores - log_total).astype(LOW)
    attended = jnp.einsum("bhqk,bkhd->bqhd", probs_low, value_vecs, preferred_element_type=F32)
    attended = attended.reshape(tokens_here, heads_here * HEAD_DIM).astype(LOW)

    cotangent_low, x_own, proj_late, router_late = lax.optimization_barrier(
        (pad_rows(cotangent.astype(LOW), padded_tokens), x_padded, proj_mine, router_weight)
    )
    cot_full = col_gather(cotangent_low)
    proj_full = col_gather(proj_late)
    router_full = lax.all_gather(router_late, "col", axis=0, tiled=True)
    x_all = row_gather(x_own)
    cot_all = row_gather(cot_full)
    cot_rows = jnp.take(cot_all, slot_token, axis=0, mode="clip").reshape(
        local_experts, row_count * CAP, full_width
    )

    attended_full = col_gather(pad_rows(attended, padded_tokens))
    attended_all = row_gather(attended_full)
    mid_all = x_all.astype(F32) + over_cols(attended_all, proj_full)
    proj_cols = lax.dynamic_slice_in_dim(
        proj_full, lax.axis_index("col") * col_width, col_width, 0
    )
    mid = block_input + over_cols(attended_full, proj_cols)[:tokens_here]
    average_two, inv_two = statistics(mid_all)
    scaled_two = (mid_all - average_two) * inv_two
    h_two = (scaled_two * gain_two + bias_two).astype(LOW)
    route_probs = jax.nn.softmax(matmul(h_two, router_full), axis=-1)
    choose = ids_all[:, :, None] == expert_range
    kept_choose = jnp.sum(jnp.where(choose, kept_all[:, :, None], 0.0), axis=1)
    gate_head, gate_tail = split_low(route_probs * kept_choose)
    side = jnp.concatenate(
        (gate_head, gate_tail, jnp.zeros((all_tokens, SIDE - 2 * E), LOW)), axis=1
    )
    table = jnp.concatenate((h_two, side), axis=1)

    slot_token = slot_token.reshape(local_experts, -1)
    slot_used = slot_used.reshape(local_experts, -1)
    step = max(1, local_experts // PARTS)
    my_experts = lax.axis_index("row") * local_experts + jnp.arange(local_experts)
    results, backs, gate_backs, grads = [], [], [], []
    for start in range(0, local_experts, step):
        part = slice(start, start + step)
        weight_in, weight_out = expert_in[part], expert_out[part]
        fetched = jnp.take(table, slot_token[part].reshape(-1), axis=0, mode="clip").reshape(
            step, row_count * CAP, -1
        )
        rows_in = fetched[:, :, :full_width]
        gate_cols = fetched[:, :, full_width:].astype(F32)
        named = (my_experts[part, None] == expert_range)[:, None, :]
        gate = jnp.sum(
            jnp.where(named, gate_cols[:, :, :E] + gate_cols[:, :, E : 2 * E], 0.0),
            axis=2,
            keepdims=True,
        )
        gate = jnp.where(slot_used[part][:, :, None], gate, 0.0)
        cot_part = cot_rows[part]
        pre = jnp.einsum("ecd,edf->ecf", rows_in, weight_in, preferred_element_type=F32)
        phi = 0.5 * (1.0 + lax.erf(pre * math.sqrt(0.5)))
        act = pre * phi
        slope = phi + pre * (jnp.exp(-0.5 * pre * pre) * (1.0 / math.sqrt(2.0 * math.pi)))
        back = jnp.einsum("ecd,efd->ecf", cot_part, weight_out, preferred_element_type=F32)
        gate_back = jnp.sum(act * back, axis=2, keepdims=True)
        pre_grad = (gate * back * slope).astype(LOW)
        act_gated = (gate * act).astype(LOW)
        input_part = jnp.einsum("ecf,edf->ecd", pre_grad, weight_in, preferred_element_type=F32)
        backs.append(input_part.astype(LOW).reshape(-1, full_width))
        gate_backs.append(jnp.broadcast_to(gate_back.reshape(-1, 1), (gate_back.size, SIDE)))
        results.append(
            jnp.einsum("ecf,efd->ecd", act_gated, weight_out, preferred_element_type=F32)
            .astype(LOW)
            .reshape(-1, full_width)
        )
        grads.append(
            (
                jnp.einsum("ecd,ecf->edf", rows_in, pre_grad, preferred_element_type=F32).astype(LOW),
                jnp.einsum("ecf,ecd->efd", act_gated, cot_part, preferred_element_type=F32).astype(LOW),
            )
        )
    backs, gate_backs, grads = lax.optimization_barrier((backs, gate_backs, grads))
    pairs = [add_beside(grad) for both in grads for grad in both]

    first, second = target.reshape(-1, 2).T

    def fetch_both(parts):
        rows = jnp.concatenate(parts + [jnp.zeros((16, parts[0].shape[1]), parts[0].dtype)])
        return [jnp.take(rows, places, axis=0, mode="clip") for places in (first, second)]

    back_first, back_second = fetch_both(backs)
    gate_first, gate_second = fetch_both(gate_backs)
    gate_grad = jnp.concatenate((gate_first[:, :1], gate_second[:, :1]), axis=1) * kept_all
    prob_grad = jnp.sum(jnp.where(choose, gate_grad[:, :, None], 0.0), axis=1)
    logit_grad = (
        route_probs * (prob_grad - jnp.sum(route_probs * prob_grad, axis=1, keepdims=True))
    ).astype(LOW)
    grad_router = over_rows(h_two, logit_grad)
    h_two_part = (
        back_first.astype(F32) + back_second.astype(F32) + over_cols(logit_grad, router_full)
    ).astype(LOW)
    h_two_part, pairs = lax.optimization_barrier((h_two_part, pairs))
    h_two_sum = col_scatter(row_reduce(h_two_part).astype(LOW))
    h_two_grad = col_gather(h_two_sum)
    early = len(pairs) // 2
    totals = [add_across(pair) for pair in pairs[:early]]
    h_two_grad, totals = lax.optimization_barrier((h_two_grad, totals))
    h_two_grad = h_two_grad[:tokens_here].astype(F32)

    result_first, result_second = fetch_both(results)
    result_part = (result_first.astype(F32) + result_second.astype(F32)).astype(LOW)
    routed = col_scatter(row_reduce(result_part).astype(LOW))[:tokens_here]
    output = mid + routed.astype(F32)

    scaled_own = scaled_two[:tokens_here]
    inv_own = inv_two[:tokens_here]
    grad_two = h_two_grad * gain_two
    norm_two_grad = inv_own * (
        grad_two
        - jnp.mean(grad_two, axis=1, keepdims=True)
        - scaled_own * jnp.mean(grad_two * scaled_own, axis=1, keepdims=True)
    )
    ln2_gain_grad = own_cols(jnp.sum(h_two_grad * scaled_own, axis=0), col_width)
    ln2_bias_grad = own_cols(jnp.sum(h_two_grad, axis=0), col_width)
    mid_full = (cot_full[:tokens_here].astype(F32) + norm_two_grad).astype(LOW)
    mid_grad = cotangent + own_cols(norm_two_grad, col_width)

    grad_proj = over_rows(mid_full, attended)
    att_grad = matmul(mid_full, proj_mine).astype(LOW)
    att_grad = att_grad.reshape(images, SEQ, heads_here, HEAD_DIM)
    scores_again = (
        jnp.einsum("bqhd,bkhd->bhqk", queries, key_vecs, preferred_element_type=F32) * score_scale
    )
    att_probs = jnp.exp(scores_again - log_total)
    prob_grads = jnp.einsum("bqhd,bkhd->bhqk", att_grad, value_vecs, preferred_element_type=F32)
    score_grad = (
        att_probs * (prob_grads - jnp.sum(att_probs * prob_grads, axis=-1, keepdims=True))
    ).astype(LOW)
    query_grad = (
        jnp.einsum("bhqk,bkhd->bqhd", score_grad, key_vecs, preferred_element_type=F32)
        * score_scale
    )
    key_grad = (
        jnp.einsum("bhqk,bqhd->bkhd", score_grad, queries, preferred_element_type=F32)
        * score_scale
    )
    value_grad = jnp.einsum(
        "bhqk,bqhd->bkhd", att_probs.astype(LOW), att_grad, preferred_element_type=F32
    )
    qkv_grad = (
        jnp.stack((query_grad, key_grad, value_grad), axis=3).reshape(tokens_here, -1).astype(LOW)
    )
    late = [add_across(pair) for pair in pairs[early:]]
    h_one_part = over_cols(qkv_grad, qkv_full).astype(LOW)
    h_one_part, totals = lax.optimization_barrier((h_one_part, totals))
    h_one_grad = col_scatter(h_one_part).astype(F32)
    for place, total in enumerate(totals + late):
        if place % 2 == 0:
            expert_in_sum = store_both(expert_in_sum, total, place // 2 * step)
        else:
            expert_out_sum = store_both(expert_out_sum, total, place // 2 * step)
    expert_in_sum = expert_in_sum.reshape(expert_in.shape)
    expert_out_sum = expert_out_sum.reshape(expert_out.shape)
    grad_qkv = over_rows(h_one_full, qkv_grad)

    scaled_full = (x_full.astype(F32) - average_one) * inv_one
    grad_one_part = h_one_part.astype(F32) * gain_one
    sums = lax.psum(
        jnp.stack((jnp.sum(grad_one_part, axis=1), jnp.sum(grad_one_part * scaled_full, axis=1))),
        "col",
    )
    grad_one = h_one_grad * ln1_gain
    norm_one_grad = inv_one * (
        grad_one
        - sums[0][:, None] / full_width
        - scaled_one * (sums[1][:, None] / full_width)
    )
    grad_input = mid_grad + norm_one_grad
    ln1_gain_grad = jnp.sum(h_one_grad * scaled_one, axis=0)
    ln1_bias_grad = jnp.sum(h_one_grad, axis=0)

    router_sum = lax.dynamic_slice_in_dim(
        lax.psum(grad_router, ("dp", "row", "col")), lax.axis_index("col") * col_width, col_width, 0
    )
    weights_sum = lax.psum(
        lax.psum_scatter(
            jnp.concatenate((grad_qkv, grad_proj), axis=1), "row", scatter_dimension=0, tiled=True
        ),
        "dp",
    )
    qkv_sum = weights_sum[:, : qkv_weight.shape[1]]
    proj_sum = weights_sum[:, qkv_weight.shape[1] :]
    vector_sums = lax.psum(
        jnp.stack((ln1_gain_grad, ln1_bias_grad, ln2_gain_grad, ln2_bias_grad)), ("dp", "row")
    )
    return (
        output,
        grad_input,
        qkv_sum,
        proj_sum,
        router_sum,
        expert_in_sum,
        expert_out_sum,
        vector_sums[0],
        vector_sums[1],
        vector_sums[2],
        vector_sums[3],
    )


def col_stats(summed, squares):
    return lax.psum((summed, squares), "col")


def col_total(values):
    return lax.psum(values, "col")


def routed_swap(values):
    return lax.all_to_all(values, "row", split_axis=0, concat_axis=0, tiled=True)


def normalize(values, gain_vec, bias_vec, full_width):
    summed, squares = col_stats(jnp.sum(values, axis=1), jnp.sum(values * values, axis=1))
    average = summed / full_width
    inv_std = lax.rsqrt(squares / full_width - average * average + EPSILON)
    scaled = (values - average[:, None]) * inv_std[:, None]
    return (scaled, inv_std, scaled * gain_vec + bias_vec)


def normalize_back(grad_out, scaled, inv_std, gain_vec, full_width):
    scaled_grad = grad_out * gain_vec
    summed, crossed = col_stats(jnp.sum(scaled_grad, axis=1), jnp.sum(scaled_grad * scaled, axis=1))
    grad_in = inv_std[:, None] * (
        scaled_grad - summed[:, None] / full_width - scaled * (crossed[:, None] / full_width)
    )
    return (grad_in, jnp.sum(grad_out * scaled, axis=0), jnp.sum(grad_out, axis=0))


def exchange_body(
    block_input,
    ln1_gain,
    ln1_bias,
    qkv_weight,
    out_weight,
    ln2_gain,
    ln2_bias,
    router_weight,
    expert_in,
    expert_out,
    expert_ids,
    kept_flags,
    cotangent,
):
    tokens_here, col_width = block_input.shape
    full_width = col_width * lax.axis_size("col")
    row_count = lax.axis_size("row")
    local_experts = expert_in.shape[0]
    images = tokens_here // SEQ
    score_scale = 1.0 / math.sqrt(HEAD_DIM)
    scaled_one, inv_one, normed_one = normalize(block_input, ln1_gain, ln1_bias, full_width)
    h_one_full = col_gather(normed_one.astype(jnp.bfloat16))
    qkv_full, proj_full = (
        lax.all_gather(qkv_weight, "row", axis=0, tiled=True),
        lax.all_gather(out_weight, "row", axis=0, tiled=True),
    )
    qkv_vals = jnp.dot(h_one_full, qkv_full, preferred_element_type=jnp.float32).astype(
        jnp.bfloat16
    )
    heads_here = qkv_vals.shape[1] // (3 * HEAD_DIM)
    qkv_grid = qkv_vals.reshape(images, SEQ, heads_here, 3, HEAD_DIM)
    queries = qkv_grid[:, :, :, 0]
    key_vecs = qkv_grid[:, :, :, 1]
    value_vecs = qkv_grid[:, :, :, 2]
    scores = (
        jnp.einsum("bqhd,bkhd->bhqk", queries, key_vecs, preferred_element_type=jnp.float32)
        * score_scale
    )
    largest = jnp.max(scores, axis=-1, keepdims=True)
    log_total = largest + jnp.log(jnp.sum(jnp.exp(scores - largest), axis=-1, keepdims=True))
    probs_low = jnp.exp(scores - log_total).astype(jnp.bfloat16)
    attended = jnp.einsum(
        "bhqk,bkhd->bqhd", probs_low, value_vecs, preferred_element_type=jnp.float32
    )
    attended = attended.reshape(tokens_here, heads_here * HEAD_DIM).astype(jnp.bfloat16)
    mid = block_input + col_scatter(over_cols(attended, proj_full))
    scaled_two, inv_two, normed_two = normalize(mid, ln2_gain, ln2_bias, full_width)
    h_two = normed_two.astype(jnp.bfloat16)
    logits = col_total(jnp.dot(h_two, router_weight, preferred_element_type=jnp.float32))
    route_probs = jax.nn.softmax(logits, axis=-1)
    expert_range = jnp.arange(E, dtype=jnp.int32)
    choose = expert_ids[:, :, None] == expert_range
    kept_vals = kept_flags.astype(jnp.float32)
    gate_vals = jnp.sum(jnp.where(choose, route_probs[:, None, :], 0.0), axis=2) * kept_vals
    flat_ids = expert_ids.reshape(-1)
    one_hot = (flat_ids[:, None] == expert_range).astype(jnp.int32)
    slot_index = jnp.sum(jnp.cumsum(one_hot, axis=0) * one_hot, axis=1) - 1
    target = flat_ids * CAP + slot_index
    route_total = flat_ids.shape[0]
    owners = (
        jnp.full((E * CAP,), route_total, jnp.int32)
        .at[target]
        .set(jnp.arange(route_total, dtype=jnp.int32))
    )
    dispatch = jnp.take(h_two, owners // 2, axis=0, mode="fill", fill_value=0)
    arrived = routed_swap(dispatch.reshape(row_count, -1, col_width))
    rows_in = col_gather(arrived.reshape(-1, col_width)).reshape(
        row_count, local_experts, CAP, full_width
    )
    first_full, second_full = (expert_in, expert_out)
    hidden_pre = jnp.einsum(
        "secd,edf->secf", rows_in, first_full, preferred_element_type=jnp.float32
    )
    hidden_act = jax.nn.gelu(hidden_pre, approximate=False).astype(jnp.bfloat16)
    expert_part = jnp.einsum(
        "secf,efd->secd", hidden_act, second_full, preferred_element_type=jnp.float32
    )
    returned = col_scatter(expert_part.reshape(-1, full_width)).astype(jnp.bfloat16)
    results = routed_swap(returned.reshape(row_count, -1, col_width)).reshape(E * CAP, col_width)
    routed = (
        jnp.take(results, target, axis=0).reshape(tokens_here, 2, col_width).astype(jnp.float32)
    )
    output = mid + jnp.sum(routed * gate_vals[:, :, None], axis=1)
    gate_grad = col_total(jnp.sum(cotangent[:, None, :] * routed, axis=2)) * kept_vals
    prob_grad = jnp.sum(jnp.where(choose, gate_grad[:, :, None], 0.0), axis=1)
    logit_grad = (
        route_probs * (prob_grad - jnp.sum(route_probs * prob_grad, axis=1, keepdims=True))
    ).astype(jnp.bfloat16)
    grad_router = over_rows(h_two, logit_grad)
    route_grad = (
        (cotangent[:, None, :] * gate_vals[:, :, None]).reshape(-1, col_width).astype(jnp.bfloat16)
    )
    grad_buffer = jnp.take(route_grad, owners, axis=0, mode="fill", fill_value=0)
    grad_arrived = routed_swap(grad_buffer.reshape(row_count, -1, col_width))
    grad_rows = col_gather(grad_arrived.reshape(-1, col_width)).reshape(
        row_count, local_experts, CAP, full_width
    )
    act_grad = jnp.einsum(
        "secd,efd->secf", grad_rows, second_full, preferred_element_type=jnp.float32
    )
    act_pullback = jax.vjp(partial(jax.nn.gelu, approximate=False), hidden_pre)[1]
    pre_grad = act_pullback(act_grad)[0].astype(jnp.bfloat16)
    grad_expert_out = jnp.einsum(
        "secf,secd->efd", hidden_act, grad_rows, preferred_element_type=jnp.float32
    )
    grad_expert_in = jnp.einsum(
        "secd,secf->edf", rows_in, pre_grad, preferred_element_type=jnp.float32
    )
    input_part = jnp.einsum(
        "secf,edf->secd", pre_grad, first_full, preferred_element_type=jnp.float32
    )
    grad_back = col_scatter(input_part.reshape(-1, full_width)).astype(jnp.bfloat16)
    grad_return = routed_swap(grad_back.reshape(row_count, -1, col_width)).reshape(
        E * CAP, col_width
    )
    grad_two_in = (
        jnp.take(grad_return, target, axis=0).reshape(tokens_here, 2, col_width).astype(jnp.float32)
    )
    h_two_grad = jnp.sum(grad_two_in, axis=1) + over_cols(logit_grad, router_weight)
    norm_two_grad, ln2_gain_grad, ln2_bias_grad = normalize_back(
        h_two_grad, scaled_two, inv_two, ln2_gain, full_width
    )
    mid_grad = cotangent + norm_two_grad
    mid_full = col_gather(mid_grad.astype(jnp.bfloat16))
    grad_proj = over_rows(mid_full, attended)
    att_grad = jnp.dot(mid_full, proj_full, preferred_element_type=jnp.float32).astype(jnp.bfloat16)
    att_grad = att_grad.reshape(images, SEQ, heads_here, HEAD_DIM)
    scores_again = (
        jnp.einsum("bqhd,bkhd->bhqk", queries, key_vecs, preferred_element_type=jnp.float32)
        * score_scale
    )
    att_probs = jnp.exp(scores_again - log_total)
    prob_grads = jnp.einsum(
        "bqhd,bkhd->bhqk", att_grad, value_vecs, preferred_element_type=jnp.float32
    )
    score_grad = (
        att_probs * (prob_grads - jnp.sum(att_probs * prob_grads, axis=-1, keepdims=True))
    ).astype(jnp.bfloat16)
    query_grad = (
        jnp.einsum("bhqk,bkhd->bqhd", score_grad, key_vecs, preferred_element_type=jnp.float32)
        * score_scale
    )
    key_grad = (
        jnp.einsum("bhqk,bqhd->bkhd", score_grad, queries, preferred_element_type=jnp.float32)
        * score_scale
    )
    value_grad = jnp.einsum(
        "bhqk,bqhd->bkhd",
        att_probs.astype(jnp.bfloat16),
        att_grad,
        preferred_element_type=jnp.float32,
    )
    qkv_grad = (
        jnp.stack((query_grad, key_grad, value_grad), axis=3)
        .reshape(tokens_here, -1)
        .astype(jnp.bfloat16)
    )
    grad_qkv = over_rows(h_one_full, qkv_grad)
    h_one_grad = col_scatter(over_cols(qkv_grad, qkv_full))
    norm_one_grad, ln1_gain_grad, ln1_bias_grad = normalize_back(
        h_one_grad, scaled_one, inv_one, ln1_gain, full_width
    )
    grad_input = mid_grad + norm_one_grad
    rows_here = qkv_weight.shape[0]
    totals_all = lax.psum(
        (
            grad_qkv,
            grad_proj,
            grad_router,
            ln1_gain_grad,
            ln1_bias_grad,
            ln2_gain_grad,
            ln2_bias_grad,
        ),
        ("dp", "row"),
    )
    row_start = lax.axis_index("row") * rows_here
    qkv_sum = lax.dynamic_slice_in_dim(totals_all[0], row_start, rows_here, 0)
    proj_sum = lax.dynamic_slice_in_dim(totals_all[1], row_start, rows_here, 0)
    router_sum = totals_all[2]
    gain_one = totals_all[3]
    bias_one = totals_all[4]
    gain_two = totals_all[5]
    bias_two = totals_all[6]
    expert_in_sum, expert_out_sum = lax.psum((grad_expert_in, grad_expert_out), "dp")
    return (
        output,
        grad_input,
        qkv_sum,
        proj_sum,
        router_sum,
        expert_in_sum,
        expert_out_sum,
        gain_one,
        bias_one,
        gain_two,
        bias_two,
    )


def solution(mesh):
    in_specs = (
        P(("dp", "row"), "col"),
        P("col"),
        P("col"),
        P("row", "col"),
        P("row", "col"),
        P("col"),
        P("col"),
        P("col", None),
        P("row", None, "col"),
        P("row", "col", None),
        P(("dp", "row"), None),
        P(("dp", "row"), None),
        P(("dp", "row"), "col"),
    )
    out_specs = (
        P(("dp", "row"), "col"),
        P(("dp", "row"), "col"),
        P("row", "col"),
        P("row", "col"),
        P("col", None),
        P("row", None, "col"),
        P("row", "col", None),
        P("col"),
        P("col"),
        P("col"),
        P("col"),
    )
    chosen = body if mesh.shape["row"] == 2 else exchange_body
    return jax.shard_map(chosen, mesh=mesh, in_specs=in_specs, out_specs=out_specs, check_vma=False)
```
